32 devices in a mesh: parts: 2 (over y), expert: 4 (over x, core), tensor: 4 (over z).
Axes of the slice: x: 2, y: 2, z: 4, core: 2. Of those that a mesh axis runs over, the one named last changes fastest.
Arguments:
- tokens: bfloat16 [32, 3072], P(('parts', 'expert', 'tensor')), parts along dimension 0, may hold values from -6 to 6
- cotangent: bfloat16 [32, 3072], P(('parts', 'expert', 'tensor')), parts along dimension 0, may hold values from -6 to 6
- routes: int32 [32, 2], P(('parts', 'expert')), parts along dimension 0, may hold values from 0 to 3, all different within a row; in each aligned block of 4 rows (0 to 3, 4 to 7, ...) at most 2 rows name the same one
- router: bfloat16 [3072, 4], replicated, may hold values from -0.109375 to 0.109375
- w_gate: bfloat16 [4, 3072, 16384], P('expert', None, 'tensor'), may hold values from -0.109375 to 0.109375
- w_up: bfloat16 [4, 3072, 16384], P('expert', None, 'tensor'), may hold values from -0.109375 to 0.109375
- w_down: bfloat16 [4, 16384, 3072], P('expert', 'tensor'), may hold values from -0.046875 to 0.046875
- adapter_down: bfloat16 [4, 3072, 32], P('expert', 'tensor'), may hold values from -0.109375 to 0.109375
- adapter_up: bfloat16 [4, 2, 16, 16384], P('expert', None, None, 'tensor'), may hold values from -1.5 to 1.5
Outputs:
- grad_tokens: bfloat16 [32, 3072], P(('parts', 'expert', 'tensor')), parts along dimension 0
- grad_down: float32 [8, 3072, 32], P(('parts', 'expert'), 'tensor'), parts along dimension 0
- grad_up: float32 [8, 2, 16, 16384], P(('parts', 'expert'), None, None, 'tensor'), parts along dimension 0
The draws below stay inside these ranges and needn't reach their ends.
There are 2 independent parts, one for each index of `parts`. The reference program is written for one: setup_inputs(seed, part) draws one part's arguments, and reference() takes and returns one part's arrays. A program takes and returns all parts, laid end to end along the dimension named above; an argument that names none is the same for every part. Nothing has to cross between parts.
Inputs may be any that keep to these rules, and one draw needn't show every extreme that they name: The two routes of a token differ. In each aligned block of 4 rows no expert is named by more than 2 routes, and some block reaches 2.
All inputs are finite; a program needn't handle non-finite values.
Results may differ from the reference program's by a relative error of at most 0.006.
Values may be sent and summed in bfloat16 or wider, within the bound.
No kernel may reach another device: no remote copies, remote signals or barrier semaphores. Data moves between devices by JAX's collectives and lax.ppermute only.
A program may use at most 192 MiB of HBM per device.

```python
import math
import jax
import jax.numpy as jnp
import numpy as np
from jax import lax

D = 3072
FF = 16384
RANK = 16
TOK_DEV = 1
EXPERTS = 4
TOKENS = 16
CAP = 2
N_EXPERT = 4
N_TENSOR = 4


def steps_of(stream_key, shape, pieces, least, largest):
    level, own = 1.0, jax.random.fold_in(stream_key, 6)
    for dim, parts in pieces:
        steps = jnp.exp(jax.random.uniform(jax.random.fold_in(own, dim), (parts,), jnp.float32, least / len(pieces), largest / len(pieces)))
        level = level * jnp.repeat(steps, shape[dim] // parts).reshape([-1 if axis == dim else 1 for axis in range(len(shape))])
    return level


def routed_block(own_key, own, number, rows, amount, top, reach, lean):
    sequence = jax.random.permutation(own_key, amount)
    heavy_load, usual = load_shares(amount, rows * top, reach, lean, True), load_shares(amount, rows * top, reach, lean, False)
    places = jnp.arange(amount)

    def named(lengths, turn):
        used = int((lengths > 0).sum())
        fixed = max(1, used // 4)
        moved = fixed + (places - fixed + turn * (used - fixed)) % max(1, amount - fixed)
        return jnp.zeros((amount,), jnp.int32).at[sequence[jnp.where(places < fixed, places, moved)]].set(jnp.asarray(lengths, jnp.int32))

    lengths = jnp.where(number % 4 == 0, named(heavy_load, number // 4), named(usual, number - number // 4 - 1))
    mixed = jax.random.permutation(jax.random.fold_in(own, 3), amount)
    giver, receiver = mixed[0:amount // 2 * 2:2], mixed[1:amount // 2 * 2:2]
    room = jnp.minimum(lengths[giver] - 1, reach - lengths[receiver]) // 2
    room = jnp.where((giver == sequence[0]) | (receiver == sequence[0]) | (lengths[receiver] == 0), 0, jnp.maximum(room, 0))
    moved = jax.random.randint(jax.random.fold_in(own, 4), (amount // 2,), 0, 1 << 20) % (room + 1)
    lengths = lengths.at[giver].add(-moved).at[receiver].add(moved)
    members = jnp.searchsorted(jnp.cumsum(lengths), jnp.arange(rows * top), side="right").astype(jnp.int32)
    grid = members.reshape(top, rows).T
    grid = grid[jax.random.permutation(jax.random.fold_in(own, 1), rows)]
    turn = jax.random.randint(jax.random.fold_in(own, 2), (rows, 1), 0, top)
    return jnp.take_along_axis(grid, (jnp.arange(top)[None, :] + turn) % top, axis=1)


def load_shares(amount, total, most, lean, full):
    portions = [(1 << 20) // math.isqrt(grade ** lean) + 1 for grade in range(1, amount + 1)]
    largest = most if full else min(most, max(-(-total // amount), total * portions[0] // sum(portions)))
    least = 1 if total - largest >= amount - 1 else 0
    given, spare = [largest] + [least] * (amount - 1), total - largest - least * (amount - 1)
    while spare > 0:
        free = [i for i in range(1, amount) if given[i] < largest] or [i for i in range(1, amount) if given[i] < most]
        mass, left = sum([portions[i] for i in free]), spare
        for i in free:
            extra = min(most - given[i], max(1, left * portions[i] // mass), spare)
            given[i] = given[i] + extra
            spare = spare - extra
    return np.array(given)


def scatter_about(stream_key, extent, width, bound, pieces=(), held_as=jnp.bfloat16):
    loudness = steps_of(stream_key, extent, pieces, -0.22, 0.18) if pieces else 1.0
    array = jax.random.normal(stream_key, extent, jnp.float32) * width * loudness
    return jnp.minimum(jnp.maximum(array, -bound), bound).astype(held_as)


def setup_inputs(seed: int = 0, part: int = 0) -> dict:
    arg_keys = jax.random.split(jax.random.key(seed), 10)
    part_keys = jax.random.split(jax.random.fold_in(arg_keys[9], part), 10)
    tokens = scatter_about(part_keys[0], (TOKENS, D), 1.0, 6.0, ((0, 16),))
    cotangent = scatter_about(part_keys[1], (TOKENS, D), 1.0, 6.0, ((0, 16),))
    routes_keys = jax.random.split(jax.random.fold_in(part_keys[2], 1), TOKENS // (TOK_DEV * N_TENSOR))
    routes_turns = jax.random.permutation(jax.random.fold_in(part_keys[2], 3), TOKENS // (TOK_DEV * N_TENSOR))
    routes = jax.vmap(lambda own, number: routed_block(jax.random.fold_in(part_keys[2], 2), own, number, TOK_DEV * N_TENSOR, EXPERTS, 2, CAP, 2))(routes_keys, routes_turns).reshape((TOKENS, 2))
    router = scatter_about(arg_keys[3], (D, EXPERTS), D ** -0.5, 0.109375)
    w_gate = scatter_about(arg_keys[4], (EXPERTS, D, FF), D ** -0.5, 0.109375, ((0, 4), (2, 4)))
    w_up = scatter_about(arg_keys[5], (EXPERTS, D, FF), D ** -0.5, 0.109375, ((0, 4), (2, 4)))
    w_down = scatter_about(arg_keys[6], (EXPERTS, FF, D), FF ** -0.5, 0.046875, ((0, 4), (1, 4)))
    adapter_down = scatter_about(arg_keys[7], (EXPERTS, D, 2 * RANK), D ** -0.5, 0.109375, ((0, 4), (1, 4)))
    adapter_up = scatter_about(arg_keys[8], (EXPERTS, 2, RANK, FF), RANK ** -0.5, 1.5, ((0, 4), (3, 4)))
    return {"tokens": tokens, "cotangent": cotangent, "routes": routes, "router": router, "w_gate": w_gate, "w_up": w_up, "w_down": w_down, "adapter_down": adapter_down, "adapter_up": adapter_up}


adapter_scale = 0.5


def slot_index(group_routes, experts, capacity):
    flat_routes = group_routes.reshape(-1)
    one_hot = (flat_routes[:, None] == jnp.arange(experts, dtype=jnp.int32)[None, :]).astype(jnp.int32)
    earlier = jnp.cumsum(one_hot, axis=0) - one_hot
    position = jnp.sum(earlier * one_hot, axis=1).astype(jnp.int32)
    return (flat_routes * capacity + position).astype(jnp.int32).reshape(group_routes.shape)


def expert_step(inputs):
    expert_rows, expert_cot, expert_gate, gate_mat, up_mat, down_mat, adapt_in, adapt_out = inputs
    latent = jnp.dot(expert_rows, adapt_in, preferred_element_type=jnp.float32).astype(jnp.bfloat16)
    latent_gate = latent[:, :RANK]
    latent_up = latent[:, RANK:]
    gate_pre = jnp.dot(expert_rows, gate_mat, preferred_element_type=jnp.float32) + adapter_scale * jnp.dot(latent_gate, adapt_out[0], preferred_element_type=jnp.float32)
    up_pre = jnp.dot(expert_rows, up_mat, preferred_element_type=jnp.float32) + adapter_scale * jnp.dot(latent_up, adapt_out[1], preferred_element_type=jnp.float32)
    sigmoid_gate = jax.nn.sigmoid(gate_pre)
    activated = gate_pre * sigmoid_gate
    hidden = activated * up_pre
    returned = lax.dot_general(expert_cot, down_mat, (((1,), (1,)), ((), ())), preferred_element_type=jnp.float32)
    d_gate_val = jnp.sum(returned * hidden, axis=1)
    d_hidden = expert_gate.astype(jnp.float32)[:, None] * returned
    d_gate_pre = (d_hidden * up_pre * sigmoid_gate * (1.0 + gate_pre * (1.0 - sigmoid_gate))).astype(jnp.bfloat16)
    d_up_pre = (d_hidden * activated).astype(jnp.bfloat16)
    contract = (((1,), (1,)), ((), ()))
    d_latent = adapter_scale * jnp.concatenate([
        lax.dot_general(d_gate_pre, adapt_out[0], contract, preferred_element_type=jnp.float32),
        lax.dot_general(d_up_pre, adapt_out[1], contract, preferred_element_type=jnp.float32)], axis=1)
    d_latent = d_latent.astype(jnp.bfloat16)
    rows_contract = (((0,), (0,)), ((), ()))
    grad_down = lax.dot_general(expert_rows, d_latent, rows_contract, preferred_element_type=jnp.float32)
    grad_up = jnp.stack([
        adapter_scale * lax.dot_general(latent_gate, d_gate_pre, rows_contract, preferred_element_type=jnp.float32),
        adapter_scale * lax.dot_general(latent_up, d_up_pre, rows_contract, preferred_element_type=jnp.float32)], axis=0)
    d_rows = lax.dot_general(d_gate_pre, gate_mat, contract, preferred_element_type=jnp.float32)
    d_rows = d_rows + lax.dot_general(d_up_pre, up_mat, contract, preferred_element_type=jnp.float32)
    d_rows = d_rows + lax.dot_general(d_latent, adapt_in, contract, preferred_element_type=jnp.float32)
    return d_rows, d_gate_val, grad_down, grad_up


def reference(tokens, cotangent, routes, router, w_gate, w_up, w_down, adapter_down, adapter_up):
    groups = N_EXPERT
    size_group = TOK_DEV * N_TENSOR
    slots_all = EXPERTS * CAP
    logits = jnp.dot(tokens, router, preferred_element_type=jnp.float32)
    picked = jnp.take_along_axis(logits, routes, axis=1)
    chance = jax.nn.sigmoid(picked[:, 0] - picked[:, 1])
    gate_vals = jnp.stack([chance, 1.0 - chance], axis=1).astype(jnp.bfloat16)
    group_routes = routes.reshape(groups, size_group, 2)
    positions = jax.vmap(lambda route_block: slot_index(route_block, EXPERTS, CAP))(group_routes)

    def fill_slots(slot_block, row_block):
        buffer = jnp.zeros((slots_all, D), jnp.bfloat16)
        buffer = buffer.at[slot_block[:, 0]].set(row_block)
        return buffer.at[slot_block[:, 1]].set(row_block)

    def fill_gates(slot_block, gate_block):
        return jnp.zeros((slots_all,), jnp.bfloat16).at[slot_block.reshape(-1)].set(gate_block.reshape(-1))

    x_buffer = jax.vmap(fill_slots)(positions, tokens.reshape(groups, size_group, D))
    cot_buffer = jax.vmap(fill_slots)(positions, cotangent.reshape(groups, size_group, D))
    gate_buffer = jax.vmap(fill_gates)(positions, gate_vals.reshape(groups, size_group, 2))

    def by_expert(buffer):
        return buffer.reshape(groups, EXPERTS, CAP, D).transpose(1, 0, 2, 3).reshape(EXPERTS, groups * CAP, D)

    gate_rows = gate_buffer.reshape(groups, EXPERTS, CAP).transpose(1, 0, 2).reshape(EXPERTS, groups * CAP)
    d_rows, d_gate_val, grad_down, grad_up = lax.map(expert_step, (by_expert(x_buffer), by_expert(cot_buffer), gate_rows, w_gate, w_up, w_down, adapter_down, adapter_up))
    d_rows = d_rows.reshape(EXPERTS, groups, CAP, D).transpose(1, 0, 2, 3).reshape(groups, slots_all, D)
    d_gate_val = d_gate_val.reshape(EXPERTS, groups, CAP).transpose(1, 0, 2).reshape(groups, slots_all)
    token_rows = jax.vmap(lambda rows_block, slot_block: jnp.take(rows_block, slot_block.reshape(-1), axis=0))(d_rows, positions)
    token_rows = token_rows.reshape(groups * size_group, 2, D).sum(axis=1)
    route_grads = jax.vmap(lambda vals, slot_block: jnp.take(vals, slot_block.reshape(-1), axis=0))(d_gate_val, positions)
    route_grads = route_grads.reshape(groups * size_group, 2)
    d_gap = (route_grads[:, 0] - route_grads[:, 1]) * chance * (1.0 - chance)
    expert_ids = jnp.arange(EXPERTS, dtype=jnp.int32)[None, :]
    d_logits = ((routes[:, 0:1] == expert_ids).astype(jnp.float32) - (routes[:, 1:2] == expert_ids).astype(jnp.float32)) * d_gap[:, None]
    grad_tokens = token_rows + jnp.dot(d_logits, router.astype(jnp.float32).T, precision=lax.Precision.HIGHEST)
    return grad_tokens.astype(jnp.bfloat16), grad_down, grad_up
```

```python
import jax
import jax.numpy as jnp
from jax import lax
from jax.experimental import pallas as pl
from jax.experimental.pallas import tpu as pltpu
from jax.sharding import PartitionSpec as P

adapter_scale = 0.5
every_axis = ("parts", "expert", "tensor")
bf16, f32 = jnp.bfloat16, jnp.float32
extra = 128
ahead = 4
vmem = pl.BlockSpec(memory_space=pltpu.VMEM)
hbm = pl.BlockSpec(memory_space=pltpu.HBM)
mib = 2**20


def dot(a, b, a_dim, b_dim):
    return lax.dot_general(a, b, (((a_dim,), (b_dim,)), ((), ())), preferred_element_type=f32)


def in_hbm(array):
    return pltpu.with_memory_space_constraint(array, pltpu.HBM)


def iota(shape, dim):
    return lax.broadcasted_iota(jnp.int32, shape, dim)


def bundle_kernel(tokens_hbm, cotangent_hbm, adapt_hbm, out, rows, sems):
    rank2, cols = adapt_hbm.shape
    copies = [
        pltpu.make_async_copy(tokens_hbm, rows.at[0], sems.at[0]),
        pltpu.make_async_copy(cotangent_hbm, rows.at[1], sems.at[1]),
        pltpu.make_async_copy(adapt_hbm, out.at[:rank2, :], sems.at[2]),
    ]
    for copy in copies:
        copy.start()
    for copy in copies:
        copy.wait()
    cuts = rows.shape[2] // cols
    cut = [
        rows[side, :, k * cols : (k + 1) * cols].astype(f32)
        for side in range(2)
        for k in range(cuts)
    ]
    rest = out.shape[0] - rank2 - 2 * cuts
    if rest:
        cut.append(jnp.zeros((rest, cols), f32))
    out[rank2:, :] = jnp.concatenate(cut, axis=0).astype(bf16)


def pack_kernel(capacity, rank2, *refs):
    routes_hbm, pieces, (out, routes, held, sems) = refs[0], refs[1:-4], refs[-4:]
    count, width = routes_hbm.shape[1], out.shape[2] - extra
    flips = len(pieces) // 2 if len(pieces) == 2 else len(pieces)
    copies = [pltpu.make_async_copy(routes_hbm, routes, sems.at[0])]
    for number, piece in enumerate(pieces):
        source = piece if flips == 1 else piece.at[rank2:, :]
        copies.append(pltpu.make_async_copy(source, held.at[number], sems.at[1 + number]))
    for copy in copies:
        copy.start()
    for copy in copies:
        copy.wait()
    own = lax.axis_index("tensor")
    experts = out.shape[0] // 2
    slots = experts * 2 * capacity
    lane, tail_row = iota((slots, count), 1), iota((count, extra), 0)
    order = jnp.zeros((slots, count), jnp.int32)
    before = jnp.zeros((count, count), jnp.int32)
    after = jnp.zeros((count, count), jnp.int32)
    first = jnp.zeros((slots, count), jnp.int32)
    second = jnp.zeros((slots, count), jnp.int32)
    tail = jnp.zeros((count, extra), jnp.int32)
    tail_lane = iota((count, extra), 1)
    for number in range(count):
        token = lax.bitwise_xor(own, number) if flips > 1 else number
        route0, route1 = routes[0, token], routes[1, token]
        first = jnp.where(lane == number, route0, first)
        second = jnp.where(lane == number, route1, second)
        before = jnp.where(iota((count, count), 0) == number, token, before)
        after = jnp.where(iota((count, count), 1) == number, token, after)
        for place, value in enumerate((route0, route1, 1, token)):
            tail = jnp.where((tail_row == number) & (tail_lane == place), value, tail)
    row = iota((slots, count), 0)
    expert = lax.div(row, 2 * capacity)
    named = (first == expert) | (second == expert)
    earlier = jnp.where(before < after, 1.0, 0.0).astype(bf16)
    position = dot(jnp.where(named, 1.0, 0.0).astype(bf16), earlier, 1, 0)
    placed = named & (position == lax.rem(row, capacity).astype(f32))
    is_token = lax.rem(row, 2 * capacity) < capacity
    take_x = jnp.where(placed & is_token, 1.0, 0.0).astype(bf16)
    take_cot = jnp.where(placed & (~is_token), 1.0, 0.0).astype(bf16)
    if flips == 1:
        x, cot = held[0], held[1]
    else:
        cols = held.shape[2]
        cuts = width // cols
        values = [held[number].astype(f32) for number in range(flips)]

        def uncut(first):
            rows = [
                jnp.concatenate([v[first + k : first + k + 1, :] for k in range(cuts)], axis=1)
                for v in values
            ]
            return jnp.concatenate(rows, axis=0).astype(bf16)

        x, cot = uncut(0), uncut(cuts)
    main = dot(take_x, x, 1, 0) + dot(take_cot, cot, 1, 0)
    tails = dot(take_x, tail.astype(f32).astype(bf16), 1, 0)
    filled = jnp.concatenate([main, tails], axis=1)
    for target in range(2 * experts):
        start = (target % experts) * 2 * capacity
        out[target] = filled[start : start + 2 * capacity, :].astype(bf16)


def spread(rank2, count):
    shape = (rank2, count * rank2)
    return (lax.rem(iota(shape, 1), rank2) == iota(shape, 0)).astype(f32).astype(bf16)


def main_kernel(sizes, *refs):
    tensor_size, expert_size, size_group, capacity, devices, tile = sizes
    (gathered, pieces, refs) = (refs[0], refs[1], refs[2:])
    (router_hbm, out_hbm, gate_hbm, up_hbm, down_hbm, out, sent, kept, own_x, own_latent) = refs[:10]
    (gate_mat, up_mat, down_mat, adapt, router, adapt_out, d_gate, d_up, d_rows, sems, small) = refs[10:]
    part, expert = lax.axis_index("parts"), lax.axis_index("expert")
    width, hidden = gate_mat.shape
    rank2 = adapt.shape[0]
    tiles = hidden // tile
    rows = d_gate.shape[0]
    part_rows = rows // 2
    rank = rank2 // 2

    copies = []
    for step in range(tiles):
        here = pl.ds(step * tile, tile)
        there = pl.ds(pl.multiple_of(part * hidden + step * tile, tile), tile)
        for side, (source, held) in enumerate(
            (
                (gate_hbm.at[0, :, there], gate_mat.at[:, here]),
                (up_hbm.at[0, :, there], up_mat.at[:, here]),
                (down_hbm.at[0, there, :], down_mat.at[here, :]),
            )
        ):
            copies.append(pltpu.make_async_copy(source, held, sems.at[side, step]))
    half_here = pl.ds(pl.multiple_of(part * hidden, hidden), hidden)
    minor = [
        pltpu.make_async_copy(router_hbm, router, small.at[0]),
        pltpu.make_async_copy(out_hbm.at[:, :, half_here], adapt_out, small.at[1]),
    ]
    if len(pieces) == 1:
        minor.append(pltpu.make_async_copy(pieces[0], adapt, small.at[2]))
    else:
        own = lax.axis_index("tensor")
        cols = pieces[0].shape[1]
        for flip, piece in enumerate(pieces):
            first = pl.multiple_of(lax.bitwise_xor(own, flip) * cols, cols)
            minor.append(
                pltpu.make_async_copy(
                    piece.at[:rank2, :], adapt.at[:, pl.ds(first, cols)], small.at[2 + flip]
                )
            )
    for copy in minor + copies[:ahead]:
        copy.start()

    def arrived(number):
        copies[number].wait()
        if number + ahead < len(copies):
            copies[number + ahead].start()

    sources = gathered.shape[0]
    slot_x = jnp.concatenate(
        [gathered[k, :capacity, :].astype(f32) for k in range(sources)], axis=0
    )
    x = slot_x[:, :width].astype(bf16)
    cot = jnp.concatenate(
        [gathered[k, capacity:, :width].astype(f32) for k in range(sources)], axis=0
    ).astype(bf16)
    route0 = slot_x[:, width : width + 1]
    route1 = slot_x[:, width + 1 : width + 2]
    used = slot_x[:, width + 2 : width + 3]
    token = slot_x[:, width + 3 : width + 4]
    expert_f = expert.astype(f32)
    group = lax.div(iota((rows, devices), 0), capacity) * size_group
    dispatch = ((iota((rows, devices), 1) - group).astype(f32) == token) & (used > 0.5)
    dispatch = jnp.where(dispatch, 1.0, 0.0).astype(bf16)
    for copy in minor:
        copy.wait()

    logits = dot(x, router[...], 1, 1)
    ids = iota(logits.shape, 1).astype(f32)
    signs = jnp.where(ids == route0, 1.0, 0.0) - jnp.where(ids == route1, 1.0, 0.0)
    chance = jax.nn.sigmoid(jnp.sum(signs * logits, axis=1, keepdims=True))
    is_first = route0 == expert_f
    gate = jnp.where(is_first, chance, 1.0 - chance).astype(bf16).astype(f32) * used
    slope = jnp.where(is_first, 1.0, -1.0) * used * chance * (1.0 - chance)

    latent = dot(x, adapt[...], 1, 1).astype(bf16)
    latent_gate, latent_up = latent[:, :rank], latent[:, rank:]

    gate_share = jnp.zeros((rows, 1), f32)
    share_gate = jnp.zeros((rows, rank), f32)
    share_up = jnp.zeros((rows, rank), f32)
    for step in range(tiles):
        here = pl.ds(step * tile, tile)
        gate_out = adapt_out[0, :, here]
        up_out = adapt_out[1, :, here]
        gate_val = adapter_scale * dot(latent_gate, gate_out, 1, 0)
        up_val = adapter_scale * dot(latent_up, up_out, 1, 0)
        arrived(3 * step)
        gate_val = gate_val + dot(x, gate_mat[:, here], 1, 0)
        arrived(3 * step + 1)
        up_val = up_val + dot(x, up_mat[:, here], 1, 0)
        arrived(3 * step + 2)
        returned = dot(cot, down_mat[here, :], 1, 1)
        sig = jax.nn.sigmoid(gate_val)
        activated = gate_val * sig
        gate_share = gate_share + jnp.sum(returned * (activated * up_val), axis=1, keepdims=True)
        d_hidden = gate * returned
        d_gate_tile = (d_hidden * up_val * sig * (1.0 + gate_val * (1.0 - sig))).astype(bf16)
        d_up_tile = (d_hidden * activated).astype(bf16)
        d_gate[:, here] = d_gate_tile
        d_up[:, here] = d_up_tile
        share_gate = share_gate + dot(d_gate_tile, gate_out, 1, 1)
        share_up = share_up + dot(d_up_tile, up_out, 1, 1)
        added = dot(d_gate_tile, gate_mat[:, here], 1, 1) + dot(d_up_tile, up_mat[:, here], 1, 1)
        if step == 0:
            d_rows[...] = added
        else:
            d_rows[...] += added
    share = adapter_scale * jnp.concatenate([share_gate, share_up], axis=1)

    high = share.astype(bf16)
    low = (share - high.astype(f32)).astype(bf16)
    all_rows = d_rows[...] + dot(high, adapt[...], 1, 0) + dot(low, adapt[...], 1, 0)
    all_rows = all_rows + (gate_share * slope) * dot(signs.astype(bf16), router[...], 1, 0)

    token_grads = dot(dispatch, all_rows.astype(bf16), 0, 0).astype(bf16)
    lanes = part_rows * rank2
    flat = dot(high, spread(rank2, part_rows), 1, 0)
    mine = lax.div(iota((rows, lanes), 1), rank2) == lax.rem(iota((rows, lanes), 0), part_rows)
    flat = jnp.where(mine, flat, 0.0).astype(bf16)
    target, source = iota((devices, rows), 0), iota((devices, rows), 1)
    to_expert = lax.rem(lax.div(target, tensor_size), expert_size) == expert
    to_part = lax.div(target, tensor_size * expert_size) == lax.div(source, part_rows)
    goes = jnp.where(to_expert & to_part, 1.0, 0.0).astype(bf16)
    latent_grads = dot(goes, flat, 1, 0).astype(bf16)
    half, half_lanes = width // 2, lanes // 2
    out[:, 0, :] = jnp.concatenate([token_grads[:, :half], latent_grads[:, :half_lanes]], axis=1)
    out[:, 1, :] = jnp.concatenate([token_grads[:, half:], latent_grads[:, half_lanes:]], axis=1)

    def of_part(array, own):
        top, bottom = array[:part_rows, :], array[part_rows:, :]
        return jnp.where((part == 0) == own, top, bottom)

    d_gate_all, d_up_all = d_gate[...].astype(f32), d_up[...].astype(f32)
    for ref, own in ((sent, False), (kept, True)):
        ref[...] = jnp.concatenate([of_part(d_gate_all, own), of_part(d_up_all, own)], 0).astype(bf16)
    own_x[...] = of_part(x.astype(f32), True).astype(bf16)
    own_latent[...] = of_part(latent.astype(f32), True).astype(bf16)


def up_kernel(kept, received, latent, out):
    part = lax.axis_index("parts")
    rows, rank2 = latent.shape
    hidden = kept.shape[1]
    rank = rank2 // 2
    for ref, number in ((kept, part), (received, 1 - part)):
        cols = pl.ds(pl.multiple_of(number * hidden, hidden), hidden)
        for side in range(2):
            out[side, :, cols] = adapter_scale * dot(
                latent[:, side * rank : (side + 1) * rank],
                ref[side * rows : (side + 1) * rows, :],
                0,
                0,
            )


def last_kernel(received, x_cols, grad_tokens, grad_down):
    rank2, cols = grad_down.shape
    width = grad_tokens.shape[1]
    half = width // 2
    if x_cols.shape[1] == cols:
        x = x_cols[...]
    else:
        x = x_cols[:, pl.ds(pl.multiple_of(lax.axis_index("tensor") * cols, cols), cols)]
    rows = x.shape[0]
    total = jnp.sum(received[...].astype(f32), axis=0)
    grad_tokens[...] = jnp.concatenate([total[0:1, :half], total[1:2, :half]], axis=1).astype(bf16)
    flat = jnp.concatenate([total[0:1, half:], total[1:2, half:]], axis=1)
    lanes = rows * rank2
    mine = lax.div(iota((rows, lanes), 1), rank2) == iota((rows, lanes), 0)
    d_latent = dot(jnp.where(mine, flat, 0.0).astype(bf16), spread(rank2, rows), 1, 1).astype(bf16)
    grad_down[...] = dot(d_latent, x, 0, 0)


def per_device(tokens, cotangent, routes, router, w_gate, w_up, w_down, adapter_down, adapter_up):
    parts, expert_size = lax.axis_size("parts"), lax.axis_size("expert")
    tensor_size = lax.axis_size("tensor")
    devices = parts * expert_size * tensor_size
    size_group, experts = routes.shape[0], router.shape[1]
    capacity = 2 * size_group // experts * 5 // 4
    width = tokens.shape[1]
    hidden = w_gate.shape[2] // parts
    rank2 = adapter_down.shape[2]
    col_width = adapter_down.shape[1]
    part_rows = expert_size * capacity
    rows = parts * part_rows
    tile = min(hidden, 512)
    tiles = hidden // tile
    lanes = part_rows * rank2

    adapt_in = adapter_down[0].T
    by_flip = tensor_size == 4 and col_width % 128 == 0

    if by_flip:
        cuts = width // col_width
        bundle_rows = rank2 + -(-2 * cuts // 16) * 16
        bundle = pl.pallas_call(
            bundle_kernel,
            out_shape=jax.ShapeDtypeStruct((bundle_rows, col_width), bf16),
            in_specs=[hbm] * 3,
            out_specs=vmem,
            scratch_shapes=[pltpu.VMEM((2, 1, width), bf16), pltpu.SemaphoreType.DMA((3,))],
            compiler_params=pltpu.CompilerParams(vmem_limit_bytes=2 * mib),
            name="bundle",
        )(in_hbm(tokens), in_hbm(cotangent), in_hbm(adapt_in))
        pieces = [bundle] + [
            lax.ppermute(bundle, "tensor", [(i, i ^ flip) for i in range(tensor_size)])
            for flip in range(1, tensor_size)
        ]
        group_rows = pieces
        held = (len(pieces), bundle_rows - rank2, col_width)
    else:
        pieces = [lax.all_gather(adapt_in, "tensor", axis=1, tiled=True)]
        group_rows = [
            lax.all_gather(rows, "tensor", axis=0, tiled=True) for rows in (tokens, cotangent)
        ]
        held = (2, size_group, width)
    packed = pl.pallas_call(
        lambda *refs: pack_kernel(capacity, rank2, *refs),
        out_shape=jax.ShapeDtypeStruct((parts * experts, 2 * capacity, width + extra), bf16),
        in_specs=[hbm] * (1 + len(group_rows)),
        out_specs=vmem,
        scratch_shapes=[
            pltpu.SMEM(routes.shape[::-1], jnp.int32),
            pltpu.VMEM(held, bf16),
            pltpu.SemaphoreType.DMA((1 + len(group_rows),)),
        ],
        compiler_params=pltpu.CompilerParams(vmem_limit_bytes=32 * mib),
        name="pack",
    )(in_hbm(routes.T), *[in_hbm(piece) for piece in group_rows])
    gathered = lax.all_to_all(packed, ("parts", "expert"), split_axis=0, concat_axis=0, tiled=True)

    sizes = (tensor_size, expert_size, size_group, capacity, devices, tile)

    def main(*refs):
        main_kernel(sizes, refs[0], refs[1 : 1 + len(pieces)], *refs[1 + len(pieces) :])

    out, sent, kept, own_x, own_latent = pl.pallas_call(
        main,
        out_shape=(
            jax.ShapeDtypeStruct((devices, 2, (width + lanes) // 2), bf16),
            jax.ShapeDtypeStruct((2 * part_rows, hidden), bf16),
            jax.ShapeDtypeStruct((2 * part_rows, hidden), bf16),
            jax.ShapeDtypeStruct((part_rows, width), bf16),
            jax.ShapeDtypeStruct((part_rows, rank2), bf16),
        ),
        in_specs=[vmem] + [hbm] * (len(pieces) + 5),
        out_specs=[vmem] * 5,
        scratch_shapes=[
            pltpu.VMEM((width, hidden), bf16),
            pltpu.VMEM((width, hidden), bf16),
            pltpu.VMEM((hidden, width), bf16),
            pltpu.VMEM((rank2, width), bf16),
            pltpu.VMEM((experts, width), bf16),
            pltpu.VMEM((2, rank2 // 2, hidden), bf16),
            pltpu.VMEM((rows, hidden), bf16),
            pltpu.VMEM((rows, hidden), bf16),
            pltpu.VMEM((rows, width), f32),
            pltpu.SemaphoreType.DMA((3, tiles)),
            pltpu.SemaphoreType.DMA((2 + len(pieces),)),
        ],
        cost_estimate=pl.CostEstimate(
            flops=10 * rows * width * hidden,
            bytes_accessed=6 * width * hidden,
            transcendentals=rows * hidden,
        ),
        compiler_params=pltpu.CompilerParams(vmem_limit_bytes=50 * mib),
        name="main",
    )(
        gathered,
        *[in_hbm(piece) for piece in pieces],
        in_hbm(router.T),
        in_hbm(adapter_up[0]),
        in_hbm(w_gate),
        in_hbm(w_up),
        in_hbm(w_down),
    )

    received = lax.all_to_all(out, every_axis, split_axis=0, concat_axis=0, tiled=True)
    other = lax.ppermute(sent, "parts", [(0, 1), (1, 0)])
    grad_up = pl.pallas_call(
        up_kernel,
        out_shape=jax.ShapeDtypeStruct(adapter_up.shape[1:], f32),
        in_specs=[vmem] * 3,
        out_specs=vmem,
        cost_estimate=pl.CostEstimate(
            flops=8 * part_rows * rank2 * hidden,
            bytes_accessed=8 * rank2 * hidden,
            transcendentals=0,
        ),
        compiler_params=pltpu.CompilerParams(vmem_limit_bytes=16 * mib),
        name="grad_up",
    )(kept, other, own_latent)

    if col_width % 128 == 0:
        x_cols = own_x
    else:
        x_cols = lax.dynamic_slice_in_dim(
            own_x, lax.axis_index("tensor") * col_width, col_width, 1
        )
    grad_tokens, grad_down = pl.pallas_call(
        last_kernel,
        out_shape=(
            jax.ShapeDtypeStruct(tokens.shape, bf16),
            jax.ShapeDtypeStruct((rank2, col_width), f32),
        ),
        in_specs=[vmem] * 2,
        out_specs=[vmem] * 2,
        compiler_params=pltpu.CompilerParams(vmem_limit_bytes=40 * mib),
        name="last",
    )(received, x_cols)
    return (grad_tokens, grad_down.T[None], grad_up[None])


def solution(mesh):
    return jax.shard_map(
        per_device,
        mesh=mesh,
        in_specs=(
            P(every_axis, None),
            P(every_axis, None),
            P(("parts", "expert"), None),
            P(),
            P("expert", None, "tensor"),
            P("expert", None, "tensor"),
            P("expert", "tensor", None),
            P("expert", "tensor", None),
            P("expert", None, None, "tensor"),
        ),
        out_specs=(
            P(every_axis, None),
            P(("parts", "expert"), "tensor", None),
            P(("parts", "expert"), None, None, "tensor"),
        ),
        check_vma=False,
    )
```

```python
import jax
import jax.numpy as jnp
from jax import lax
from jax.experimental import pallas as pl
from jax.experimental.pallas import tpu as pltpu
from jax.sharding import PartitionSpec as P

adapter_scale = 0.5
every_axis = ("parts", "expert", "tensor")
bf16, f32 = jnp.bfloat16, jnp.float32
extra = 128
ahead = 2
vmem = pl.BlockSpec(memory_space=pltpu.VMEM)
hbm = pl.BlockSpec(memory_space=pltpu.HBM)
mib = 2**20


def dot(a, b, a_dim, b_dim):
    return lax.dot_general(a, b, (((a_dim,), (b_dim,)), ((), ())), preferred_element_type=f32)


def in_hbm(array):
    return pltpu.with_memory_space_constraint(array, pltpu.HBM)


def iota(shape, dim):
    return lax.broadcasted_iota(jnp.int32, shape, dim)


def bundle_kernel(tokens_hbm, cotangent_hbm, adapt_hbm, out, rows, sems):
    rank2, cols = adapt_hbm.shape
    copies = [
        pltpu.make_async_copy(tokens_hbm, rows.at[0], sems.at[0]),
        pltpu.make_async_copy(cotangent_hbm, rows.at[1], sems.at[1]),
        pltpu.make_async_copy(adapt_hbm, out.at[:rank2, :], sems.at[2]),
    ]
    for copy in copies:
        copy.start()
    for copy in copies:
        copy.wait()
    cuts = rows.shape[2] // cols
    cut = [
        rows[side, :, k * cols : (k + 1) * cols].astype(f32)
        for side in range(2)
        for k in range(cuts)
    ]
    rest = out.shape[0] - rank2 - 2 * cuts
    if rest:
        cut.append(jnp.zeros((rest, cols), f32))
    out[rank2:, :] = jnp.concatenate(cut, axis=0).astype(bf16)


def pack_kernel(capacity, rank2, flips, routes_hbm, *refs):
    pieces, (outs, adapt, routes, sem) = refs[:-4], refs[-4:]
    count, width = routes_hbm.shape[1], adapt.shape[1]
    copy = pltpu.make_async_copy(routes_hbm, routes, sem)
    copy.start()
    own = lax.axis_index("tensor")
    if flips == 1:
        x, cot = pieces[0][...], pieces[1][...]
        adapt[...] = pieces[2][...]
    else:
        cols = pieces[0].shape[1]
        cuts = width // cols
        values = [piece[rank2:, :].astype(f32) for piece in pieces]

        def uncut(first):
            rows = [
                jnp.concatenate([v[first + k : first + k + 1, :] for k in range(cuts)], axis=1)
                for v in values
            ]
            return jnp.concatenate(rows, axis=0).astype(bf16)

        x, cot = uncut(0), uncut(cuts)
        for flip, piece in enumerate(pieces):
            first = pl.multiple_of(lax.bitwise_xor(own, flip) * cols, cols)
            adapt[:, pl.ds(first, cols)] = piece[:rank2, :]
    copy.wait()
    experts = len(outs)
    slots = experts * 2 * capacity
    lane, tail_row = iota((slots, count), 1), iota((count, extra), 0)
    before = jnp.zeros((count, count), jnp.int32)
    after = jnp.zeros((count, count), jnp.int32)
    first = jnp.zeros((slots, count), jnp.int32)
    second = jnp.zeros((slots, count), jnp.int32)
    tail = jnp.zeros((count, extra), jnp.int32)
    tail_lane = iota((count, extra), 1)
    for number in range(count):
        token = lax.bitwise_xor(own, number) if flips > 1 else number
        route0, route1 = routes[0, token], routes[1, token]
        first = jnp.where(lane == number, route0, first)
        second = jnp.where(lane == number, route1, second)
        before = jnp.where(iota((count, count), 0) == number, token, before)
        after = jnp.where(iota((count, count), 1) == number, token, after)
        for place, value in enumerate((route0, route1, 1, token)):
            tail = jnp.where((tail_row == number) & (tail_lane == place), value, tail)
    row = iota((slots, count), 0)
    expert = lax.bitwise_xor(lax.div(row, 2 * capacity), lax.axis_index("expert"))
    named = (first == expert) | (second == expert)
    earlier = jnp.where(before < after, 1.0, 0.0).astype(bf16)
    position = dot(jnp.where(named, 1.0, 0.0).astype(bf16), earlier, 1, 0)
    placed = named & (position == lax.rem(row, capacity).astype(f32))
    is_token = lax.rem(row, 2 * capacity) < capacity
    take_x = jnp.where(placed & is_token, 1.0, 0.0).astype(bf16)
    take_cot = jnp.where(placed & (~is_token), 1.0, 0.0).astype(bf16)
    main = dot(take_x, x, 1, 0) + dot(take_cot, cot, 1, 0)
    tails = dot(take_x, tail.astype(f32).astype(bf16), 1, 0)
    filled = jnp.concatenate([main, tails], axis=1)
    for number, out in enumerate(outs):
        start = number * 2 * capacity
        out[...] = filled[start : start + 2 * capacity, :].astype(bf16)


def fetch_kernel(weights, out, sem):
    hidden = out.shape[1]
    there = pl.ds(pl.multiple_of(lax.axis_index("parts") * hidden, hidden), hidden)
    copy = pltpu.make_async_copy(weights.at[0, :, there], out, sem)
    copy.start()
    copy.wait()


def fetch(weights, hidden):
    width = weights.shape[1]
    return pl.pallas_call(
        fetch_kernel,
        out_shape=pltpu.VMEM((width, hidden), bf16),
        in_specs=[hbm],
        out_specs=vmem,
        scratch_shapes=[pltpu.SemaphoreType.DMA],
        cost_estimate=pl.CostEstimate(
            flops=0, bytes_accessed=4 * width * hidden, transcendentals=0
        ),
        compiler_params=pltpu.CompilerParams(vmem_limit_bytes=mib),
        name="fetch",
    )(in_hbm(weights))


def spread(rank2, count):
    shape = (rank2, count * rank2)
    return (lax.rem(iota(shape, 1), rank2) == iota(shape, 0)).astype(f32).astype(bf16)


def main_kernel(sizes, *refs):
    tensor_size, expert_size, size_group, capacity, devices, tile = sizes
    slots, adapt, gate_mat, router_hbm, out_hbm, up_hbm, down_hbm = refs[:7]
    out, sent, kept, own_x, own_latent = refs[7:12]
    up_mat, down_mat, router, adapt_out, gate_pre, d_gate, d_up, d_rows, sems, small = refs[12:]
    part, expert = lax.axis_index("parts"), lax.axis_index("expert")
    width, hidden = gate_mat.shape
    rank2 = adapt.shape[0]
    tiles = hidden // tile
    rows = d_gate.shape[0]
    part_rows = rows // 2
    rank = rank2 // 2

    copies = []
    for step in range(tiles):
        here = pl.ds(step * tile, tile)
        there = pl.ds(pl.multiple_of(part * hidden + step * tile, tile), tile)
        for side, (source, held) in enumerate(
            (
                (up_hbm.at[0, :, there], up_mat.at[:, here]),
                (down_hbm.at[0, there, :], down_mat.at[here, :]),
            )
        ):
            copies.append(pltpu.make_async_copy(source, held, sems.at[side, step]))

    def arrived(number):
        copies[number].wait()
        if number + ahead < len(copies):
            copies[number + ahead].start()

    half_here = pl.ds(pl.multiple_of(part * hidden, hidden), hidden)
    minor = [
        pltpu.make_async_copy(router_hbm, router, small.at[0]),
        pltpu.make_async_copy(out_hbm.at[:, :, half_here], adapt_out, small.at[1]),
    ]
    for copy in minor + copies[:ahead]:
        copy.start()

    held = [ref[...].astype(f32) for ref in slots]
    slot_x = jnp.concatenate([rows_of[:capacity] for rows_of in held], axis=0)
    x = slot_x[:, :width].astype(bf16)
    cot = jnp.concatenate([rows_of[capacity:, :width] for rows_of in held], axis=0).astype(bf16)
    route0 = slot_x[:, width : width + 1]
    route1 = slot_x[:, width + 1 : width + 2]
    used = slot_x[:, width + 2 : width + 3]
    token = slot_x[:, width + 3 : width + 4]
    expert_f = expert.astype(f32)
    slot_id = iota((rows, devices), 0)
    source = lax.bitwise_xor(lax.div(lax.rem(slot_id, part_rows), capacity), expert)
    slot_part = jnp.where(slot_id < part_rows, part, 1 - part)
    group = (slot_part * expert_size + source) * size_group
    dispatch = ((iota((rows, devices), 1) - group).astype(f32) == token) & (used > 0.5)
    dispatch = jnp.where(dispatch, 1.0, 0.0).astype(bf16)
    for copy in minor:
        copy.wait()

    logits = dot(x, router[...], 1, 1)
    ids = iota(logits.shape, 1).astype(f32)
    signs = jnp.where(ids == route0, 1.0, 0.0) - jnp.where(ids == route1, 1.0, 0.0)
    chance = jax.nn.sigmoid(jnp.sum(signs * logits, axis=1, keepdims=True))
    is_first = route0 == expert_f
    gate = jnp.where(is_first, chance, 1.0 - chance).astype(bf16).astype(f32) * used
    slope = jnp.where(is_first, 1.0, -1.0) * used * chance * (1.0 - chance)

    latent = dot(x, adapt[...], 1, 1).astype(bf16)
    latent_gate, latent_up = latent[:, :rank], latent[:, rank:]

    wide = min(hidden, 1024)
    for step in range(hidden // wide):
        here = pl.ds(step * wide, wide)
        gate_pre[:, here] = dot(x, gate_mat[:, here], 1, 0) + adapter_scale * dot(
            latent_gate, adapt_out[0, :, here], 1, 0
        )
    gate_share = jnp.zeros((rows, 1), f32)
    share_gate = jnp.zeros((rows, rank), f32)
    share_up = jnp.zeros((rows, rank), f32)
    for step in range(tiles):
        here = pl.ds(step * tile, tile)
        gate_val = gate_pre[:, here]
        up_val = adapter_scale * dot(latent_up, adapt_out[1, :, here], 1, 0)
        arrived(2 * step)
        up_val = up_val + dot(x, up_mat[:, here], 1, 0)
        arrived(2 * step + 1)
        returned = dot(cot, down_mat[here, :], 1, 1)
        sig = jax.nn.sigmoid(gate_val)
        activated = gate_val * sig
        gate_share = gate_share + jnp.sum(returned * (activated * up_val), axis=1, keepdims=True)
        d_hidden = gate * returned
        d_gate_tile = (d_hidden * up_val * sig * (1.0 + gate_val * (1.0 - sig))).astype(bf16)
        d_up_tile = (d_hidden * activated).astype(bf16)
        d_gate[:, here] = d_gate_tile
        d_up[:, here] = d_up_tile
        share_gate = share_gate + dot(d_gate_tile, adapt_out[0, :, here], 1, 1)
        share_up = share_up + dot(d_up_tile, adapt_out[1, :, here], 1, 1)
        added = dot(d_gate_tile, gate_mat[:, here], 1, 1) + dot(d_up_tile, up_mat[:, here], 1, 1)
        if step == 0:
            d_rows[...] = added
        else:
            d_rows[...] += added
    share = adapter_scale * jnp.concatenate([share_gate, share_up], axis=1)

    high = share.astype(bf16)
    low = (share - high.astype(f32)).astype(bf16)
    all_rows = d_rows[...] + dot(high, adapt[...], 1, 0) + dot(low, adapt[...], 1, 0)
    all_rows = all_rows + (gate_share * slope) * dot(signs.astype(bf16), router[...], 1, 0)

    token_grads = dot(dispatch, all_rows.astype(bf16), 0, 0).astype(bf16)
    lanes = part_rows * rank2
    flat = dot(high, spread(rank2, part_rows), 1, 0)
    mine = lax.div(iota((rows, lanes), 1), rank2) == lax.rem(iota((rows, lanes), 0), part_rows)
    flat = jnp.where(mine, flat, 0.0).astype(bf16)
    target, source = iota((devices, rows), 0), iota((devices, rows), 1)
    to_expert = lax.rem(lax.div(target, tensor_size), expert_size) == expert
    source_part = jnp.where(source < part_rows, part, 1 - part)
    to_part = lax.div(target, tensor_size * expert_size) == source_part
    goes = jnp.where(to_expert & to_part, 1.0, 0.0).astype(bf16)
    latent_grads = dot(goes, flat, 1, 0).astype(bf16)
    half, half_lanes = width // 2, lanes // 2
    out[:, 0, :] = jnp.concatenate([token_grads[:, :half], latent_grads[:, :half_lanes]], axis=1)
    out[:, 1, :] = jnp.concatenate([token_grads[:, half:], latent_grads[:, half_lanes:]], axis=1)

    d_gate_all, d_up_all = d_gate[...].astype(f32), d_up[...].astype(f32)
    for ref, first in ((kept, 0), (sent, part_rows)):
        rows_of = slice(first, first + part_rows)
        ref[...] = jnp.concatenate([d_gate_all[rows_of], d_up_all[rows_of]], axis=0).astype(bf16)
    own_x[...] = slot_x[:part_rows, :width].astype(bf16)
    own_latent[...] = latent.astype(f32)[:part_rows].astype(bf16)


def up_kernel(kept, received, latent, out):
    part = lax.axis_index("parts")
    rows, rank2 = latent.shape
    hidden = kept.shape[1]
    rank = rank2 // 2
    for ref, number in ((kept, part), (received, 1 - part)):
        cols = pl.ds(pl.multiple_of(number * hidden, hidden), hidden)
        for side in range(2):
            out[side, :, cols] = adapter_scale * dot(
                latent[:, side * rank : (side + 1) * rank],
                ref[side * rows : (side + 1) * rows, :],
                0,
                0,
            )


def last_kernel(received, x_cols, grad_tokens, grad_down):
    rank2, cols = grad_down.shape
    width = grad_tokens.shape[1]
    half = width // 2
    if x_cols.shape[1] == cols:
        x = x_cols[...]
    else:
        x = x_cols[:, pl.ds(pl.multiple_of(lax.axis_index("tensor") * cols, cols), cols)]
    rows = x.shape[0]
    total = jnp.sum(received[...].astype(f32), axis=0)
    grad_tokens[...] = jnp.concatenate([total[0:1, :half], total[1:2, :half]], axis=1).astype(bf16)
    flat = jnp.concatenate([total[0:1, half:], total[1:2, half:]], axis=1)
    lanes = rows * rank2
    mine = lax.div(iota((rows, lanes), 1), rank2) == iota((rows, lanes), 0)
    d_latent = dot(jnp.where(mine, flat, 0.0).astype(bf16), spread(rank2, rows), 1, 1).astype(bf16)
    grad_down[...] = dot(d_latent, x, 0, 0)


def per_device(tokens, cotangent, routes, router, w_gate, w_up, w_down, adapter_down, adapter_up):
    parts, expert_size = lax.axis_size("parts"), lax.axis_size("expert")
    tensor_size = lax.axis_size("tensor")
    devices = parts * expert_size * tensor_size
    size_group, experts = routes.shape[0], router.shape[1]
    capacity = 2 * size_group // experts * 5 // 4
    width = tokens.shape[1]
    hidden = w_gate.shape[2] // parts
    rank2 = adapter_down.shape[2]
    col_width = adapter_down.shape[1]
    part_rows = expert_size * capacity
    rows = parts * part_rows
    tile = min(hidden, 512)
    tiles = hidden // tile
    lanes = part_rows * rank2

    adapt_in = adapter_down[0].T
    by_flip = tensor_size == 4 and col_width % 128 == 0

    if by_flip:
        cuts = width // col_width
        bundle_rows = rank2 + -(-2 * cuts // 16) * 16
        bundle = pl.pallas_call(
            bundle_kernel,
            out_shape=jax.ShapeDtypeStruct((bundle_rows, col_width), bf16),
            in_specs=[hbm] * 3,
            out_specs=vmem,
            scratch_shapes=[pltpu.VMEM((2, 1, width), bf16), pltpu.SemaphoreType.DMA((3,))],
            compiler_params=pltpu.CompilerParams(vmem_limit_bytes=2 * mib),
            name="bundle",
        )(in_hbm(tokens), in_hbm(cotangent), in_hbm(adapt_in))
        pieces = [bundle] + [
            lax.ppermute(bundle, "tensor", [(i, i ^ flip) for i in range(tensor_size)])
            for flip in range(1, tensor_size)
        ]
        group_rows = pieces
    else:
        pieces = [lax.all_gather(adapt_in, "tensor", axis=1, tiled=True)]
        group_rows = [
            lax.all_gather(rows, "tensor", axis=0, tiled=True) for rows in (tokens, cotangent)
        ] + pieces
    gate_half = fetch(w_gate, hidden)

    def pack(*refs):
        inputs, outputs = refs[: 1 + len(group_rows)], refs[2 + len(group_rows) :]
        pack_kernel(
            capacity, rank2, len(pieces), *inputs, outputs[:experts], *outputs[experts:]
        )

    *packed, adapt = pl.pallas_call(
        pack,
        out_shape=(
            *(jax.ShapeDtypeStruct((2 * capacity, width + extra), bf16),) * experts,
            jax.ShapeDtypeStruct((rank2, width), bf16),
        ),
        in_specs=[hbm] + [vmem] * (1 + len(group_rows)),
        out_specs=[vmem] * (experts + 1),
        scratch_shapes=[
            pltpu.SMEM(routes.shape[::-1], jnp.int32),
            pltpu.SemaphoreType.DMA,
        ],
        compiler_params=pltpu.CompilerParams(vmem_limit_bytes=16 * mib),
        name="pack",
    )(in_hbm(routes.T), *group_rows, pltpu.with_memory_space_constraint(gate_half, pltpu.VMEM))
    plane = range(parts * experts)
    slots = [packed[0]] + [
        lax.ppermute(packed[flip % experts], ("parts", "expert"), [(i, i ^ flip) for i in plane])
        for flip in plane
        if flip > 0
    ]
    sizes = (tensor_size, expert_size, size_group, capacity, devices, tile)

    def main(*refs):
        main_kernel(sizes, refs[: len(slots)], *refs[len(slots) :])

    out, sent, kept, own_x, own_latent = pl.pallas_call(
        main,
        out_shape=(
            jax.ShapeDtypeStruct((devices, 2, (width + lanes) // 2), bf16),
            jax.ShapeDtypeStruct((2 * part_rows, hidden), bf16),
            jax.ShapeDtypeStruct((2 * part_rows, hidden), bf16),
            jax.ShapeDtypeStruct((part_rows, width), bf16),
            jax.ShapeDtypeStruct((part_rows, rank2), bf16),
        ),
        in_specs=[vmem] * (len(slots) + 2) + [hbm] * 4,
        out_specs=[vmem] * 5,
        scratch_shapes=[
            pltpu.VMEM((width, hidden), bf16),
            pltpu.VMEM((hidden, width), bf16),
            pltpu.VMEM((experts, width), bf16),
            pltpu.VMEM((2, rank2 // 2, hidden), bf16),
            pltpu.VMEM((rows, hidden), f32),
            pltpu.VMEM((rows, hidden), bf16),
            pltpu.VMEM((rows, hidden), bf16),
            pltpu.VMEM((rows, width), f32),
            pltpu.SemaphoreType.DMA((2, tiles)),
            pltpu.SemaphoreType.DMA((2,)),
        ],
        cost_estimate=pl.CostEstimate(
            flops=10 * rows * width * hidden,
            bytes_accessed=2 * width * hidden,
            transcendentals=rows * hidden,
        ),
        compiler_params=pltpu.CompilerParams(vmem_limit_bytes=38 * mib),
        name="main",
    )(
        *slots,
        adapt,
        pltpu.with_memory_space_constraint(gate_half, pltpu.VMEM),
        in_hbm(router.T),
        in_hbm(adapter_up[0]),
        in_hbm(w_up),
        in_hbm(w_down),
    )

    received = lax.all_to_all(out, every_axis, split_axis=0, concat_axis=0, tiled=True)
    other = lax.ppermute(sent, "parts", [(0, 1), (1, 0)])
    grad_up = pl.pallas_call(
        up_kernel,
        out_shape=jax.ShapeDtypeStruct(adapter_up.shape[1:], f32),
        in_specs=[vmem] * 3,
        out_specs=vmem,
        cost_estimate=pl.CostEstimate(
            flops=8 * part_rows * rank2 * hidden,
            bytes_accessed=8 * rank2 * hidden,
            transcendentals=0,
        ),
        compiler_params=pltpu.CompilerParams(vmem_limit_bytes=16 * mib),
        name="grad_up",
    )(kept, other, own_latent)

    if col_width % 128 == 0:
        x_cols = own_x
    else:
        x_cols = lax.dynamic_slice_in_dim(
            own_x, lax.axis_index("tensor") * col_width, col_width, 1
        )
    grad_tokens, grad_down = pl.pallas_call(
        last_kernel,
        out_shape=(
            jax.ShapeDtypeStruct(tokens.shape, bf16),
            jax.ShapeDtypeStruct((rank2, col_width), f32),
        ),
        in_specs=[vmem] * 2,
        out_specs=[vmem] * 2,
        compiler_params=pltpu.CompilerParams(vmem_limit_bytes=40 * mib),
        name="last",
    )(received, x_cols)
    return (grad_tokens, grad_down.T[None], grad_up[None])


def solution(mesh):
    return jax.shard_map(
        per_device,
        mesh=mesh,
        in_specs=(
            P(every_axis, None),
            P(every_axis, None),
            P(("parts", "expert"), None),
            P(),
            P("expert", None, "tensor"),
            P("expert", None, "tensor"),
            P("expert", "tensor", None),
            P("expert", "tensor", None),
            P("expert", None, None, "tensor"),
        ),
        out_specs=(
            P(every_axis, None),
            P(("parts", "expert"), "tensor", None),
            P(("parts", "expert"), None, None, "tensor"),
        ),
        check_vma=False,
    )
```

```python
import jax
import jax.numpy as jnp
from jax import lax
from jax.experimental import pallas as pl
from jax.experimental.pallas import tpu as pltpu
from jax.sharding import PartitionSpec as P

adapter_scale = 0.5
every_axis = ("parts", "expert", "tensor")
bf16, f32 = jnp.bfloat16, jnp.float32
extra = 128
ahead = 2
vmem = pl.BlockSpec(memory_space=pltpu.VMEM)
hbm = pl.BlockSpec(memory_space=pltpu.HBM)
mib = 2**20


def dot(a, b, a_dim, b_dim):
    return lax.dot_general(a, b, (((a_dim,), (b_dim,)), ((), ())), preferred_element_type=f32)


def in_hbm(array):
    return pltpu.with_memory_space_constraint(array, pltpu.HBM)


def iota(shape, dim):
    return lax.broadcasted_iota(jnp.int32, shape, dim)


def bundle_kernel(tokens_hbm, cotangent_hbm, adapt_hbm, out, rows, sems):
    rank2, cols = adapt_hbm.shape
    copies = [
        pltpu.make_async_copy(tokens_hbm, rows.at[0], sems.at[0]),
        pltpu.make_async_copy(cotangent_hbm, rows.at[1], sems.at[1]),
        pltpu.make_async_copy(adapt_hbm, out.at[:rank2, :], sems.at[2]),
    ]
    for copy in copies:
        copy.start()
    for copy in copies:
        copy.wait()
    cuts = rows.shape[2] // cols
    cut = [
        rows[side, :, k * cols : (k + 1) * cols].astype(f32)
        for side in range(2)
        for k in range(cuts)
    ]
    rest = out.shape[0] - rank2 - 2 * cuts
    if rest:
        cut.append(jnp.zeros((rest, cols), f32))
    out[rank2:, :] = jnp.concatenate(cut, axis=0).astype(bf16)


def pack_kernel(capacity, rank2, flips, routes_hbm, *refs):
    pieces, (outs, adapt, routes, sem) = refs[:-4], refs[-4:]
    count, width = routes_hbm.shape[1], adapt.shape[1]
    copy = pltpu.make_async_copy(routes_hbm, routes, sem)
    copy.start()
    own = lax.axis_index("tensor")
    if flips == 1:
        x, cot = pieces[0][...], pieces[1][...]
        adapt[...] = pieces[2][...]
    else:
        cols = pieces[0].shape[1]
        cuts = width // cols
        values = [piece[rank2:, :].astype(f32) for piece in pieces]

        def uncut(first):
            rows = [
                jnp.concatenate([v[first + k : first + k + 1, :] for k in range(cuts)], axis=1)
                for v in values
            ]
            return jnp.concatenate(rows, axis=0).astype(bf16)

        x, cot = uncut(0), uncut(cuts)
        for flip, piece in enumerate(pieces):
            first = pl.multiple_of(lax.bitwise_xor(own, flip) * cols, cols)
            adapt[:, pl.ds(first, cols)] = piece[:rank2, :]
    copy.wait()
    experts = len(outs)
    slots = experts * 2 * capacity
    lane, tail_row = iota((slots, count), 1), iota((count, extra), 0)
    before = jnp.zeros((count, count), jnp.int32)
    after = jnp.zeros((count, count), jnp.int32)
    first = jnp.zeros((slots, count), jnp.int32)
    second = jnp.zeros((slots, count), jnp.int32)
    tail = jnp.zeros((count, extra), jnp.int32)
    tail_lane = iota((count, extra), 1)
    for number in range(count):
        token = lax.bitwise_xor(own, number) if flips > 1 else number
        route0, route1 = routes[0, token], routes[1, token]
        first = jnp.where(lane == number, route0, first)
        second = jnp.where(lane == number, route1, second)
        before = jnp.where(iota((count, count), 0) == number, token, before)
        after = jnp.where(iota((count, count), 1) == number, token, after)
        for place, value in enumerate((route0, route1, 1, token)):
            tail = jnp.where((tail_row == number) & (tail_lane == place), value, tail)
    row = iota((slots, count), 0)
    expert = lax.bitwise_xor(lax.div(row, 2 * capacity), lax.axis_index("expert"))
    named = (first == expert) | (second == expert)
    earlier = jnp.where(before < after, 1.0, 0.0).astype(bf16)
    position = dot(jnp.where(named, 1.0, 0.0).astype(bf16), earlier, 1, 0)
    placed = named & (position == lax.rem(row, capacity).astype(f32))
    is_token = lax.rem(row, 2 * capacity) < capacity
    take_x = jnp.where(placed & is_token, 1.0, 0.0).astype(bf16)
    take_cot = jnp.where(placed & (~is_token), 1.0, 0.0).astype(bf16)
    main = dot(take_x, x, 1, 0) + dot(take_cot, cot, 1, 0)
    tails = dot(take_x, tail.astype(f32).astype(bf16), 1, 0)
    filled = jnp.concatenate([main, tails], axis=1)
    for number, out in enumerate(outs):
        start = number * 2 * capacity
        out[...] = filled[start : start + 2 * capacity, :].astype(bf16)


def fetch_kernel(weights, router, adapt_out, out, router_to, adapt_out_to, sems):
    hidden = out.shape[1]
    there = pl.ds(pl.multiple_of(lax.axis_index("parts") * hidden, hidden), hidden)
    copies = [
        pltpu.make_async_copy(weights.at[0, :, there], out, sems.at[0]),
        pltpu.make_async_copy(router, router_to, sems.at[1]),
        pltpu.make_async_copy(adapt_out.at[:, :, there], adapt_out_to, sems.at[2]),
    ]
    for copy in copies:
        copy.start()
    for copy in copies:
        copy.wait()


def fetch(weights, router, adapt_out, hidden):
    width = weights.shape[1]
    return pl.pallas_call(
        fetch_kernel,
        out_shape=(
            pltpu.VMEM((width, hidden), bf16),
            pltpu.VMEM(router.shape, bf16),
            pltpu.VMEM((*adapt_out.shape[:2], hidden), bf16),
        ),
        in_specs=[hbm] * 3,
        out_specs=[vmem] * 3,
        scratch_shapes=[pltpu.SemaphoreType.DMA((3,))],
        cost_estimate=pl.CostEstimate(
            flops=0, bytes_accessed=4 * width * hidden, transcendentals=0
        ),
        compiler_params=pltpu.CompilerParams(vmem_limit_bytes=mib),
        name="fetch",
    )(in_hbm(weights), in_hbm(router), in_hbm(adapt_out))


def spread(rank2, count):
    shape = (rank2, count * rank2)
    return (lax.rem(iota(shape, 1), rank2) == iota(shape, 0)).astype(f32).astype(bf16)


def main_kernel(sizes, *refs):
    tensor_size, expert_size, size_group, capacity, devices, tile = sizes
    slots, adapt, gate_mat, router, adapt_out, up_hbm, down_hbm = refs[:7]
    out, sent, kept, own_x, own_latent = refs[7:12]
    up_mat, down_mat, gate_pre, d_gate, d_up, d_rows, sems = refs[12:]
    part, expert = lax.axis_index("parts"), lax.axis_index("expert")
    width, hidden = gate_mat.shape
    rank2 = adapt.shape[0]
    tiles = hidden // tile
    rows = d_gate.shape[0]
    part_rows = rows // 2
    rank = rank2 // 2

    copies = []
    for step in range(tiles):
        here = pl.ds(step * tile, tile)
        there = pl.ds(pl.multiple_of(part * hidden + step * tile, tile), tile)
        for side, (source, held) in enumerate(
            (
                (up_hbm.at[0, :, there], up_mat.at[:, here]),
                (down_hbm.at[0, there, :], down_mat.at[here, :]),
            )
        ):
            copies.append(pltpu.make_async_copy(source, held, sems.at[side, step]))

    def arrived(number):
        copies[number].wait()
        if number + ahead < len(copies):
            copies[number + ahead].start()

    for copy in copies[:ahead]:
        copy.start()

    held = [ref[...].astype(f32) for ref in slots]
    slot_x = jnp.concatenate([rows_of[:capacity] for rows_of in held], axis=0)
    x = slot_x[:, :width].astype(bf16)
    cot = jnp.concatenate([rows_of[capacity:, :width] for rows_of in held], axis=0).astype(bf16)
    route0 = slot_x[:, width : width + 1]
    route1 = slot_x[:, width + 1 : width + 2]
    used = slot_x[:, width + 2 : width + 3]
    token = slot_x[:, width + 3 : width + 4]
    expert_f = expert.astype(f32)
    slot_id = iota((rows, devices), 0)
    source = lax.bitwise_xor(lax.div(lax.rem(slot_id, part_rows), capacity), expert)
    slot_part = jnp.where(slot_id < part_rows, part, 1 - part)
    group = (slot_part * expert_size + source) * size_group
    dispatch = ((iota((rows, devices), 1) - group).astype(f32) == token) & (used > 0.5)
    dispatch = jnp.where(dispatch, 1.0, 0.0).astype(bf16)
    logits = dot(x, router[...], 1, 1)
    ids = iota(logits.shape, 1).astype(f32)
    signs = jnp.where(ids == route0, 1.0, 0.0) - jnp.where(ids == route1, 1.0, 0.0)
    chance = jax.nn.sigmoid(jnp.sum(signs * logits, axis=1, keepdims=True))
    is_first = route0 == expert_f
    gate = jnp.where(is_first, chance, 1.0 - chance).astype(bf16).astype(f32) * used
    slope = jnp.where(is_first, 1.0, -1.0) * used * chance * (1.0 - chance)

    latent = dot(x, adapt[...], 1, 1).astype(bf16)
    latent_gate, latent_up = latent[:, :rank], latent[:, rank:]

    wide = min(hidden, 1024)
    for step in range(hidden // wide):
        here = pl.ds(step * wide, wide)
        gate_pre[:, here] = dot(x, gate_mat[:, here], 1, 0) + adapter_scale * dot(
            latent_gate, adapt_out[0, :, here], 1, 0
        )
    gate_share = jnp.zeros((rows, 1), f32)
    share_gate = jnp.zeros((rows, rank), f32)
    share_up = jnp.zeros((rows, rank), f32)
    for step in range(tiles):
        here = pl.ds(step * tile, tile)
        gate_val = gate_pre[:, here]
        up_val = adapter_scale * dot(latent_up, adapt_out[1, :, here], 1, 0)
        arrived(2 * step)
        up_val = up_val + dot(x, up_mat[:, here], 1, 0)
        arrived(2 * step + 1)
        returned = dot(cot, down_mat[here, :], 1, 1)
        sig = jax.nn.sigmoid(gate_val)
        activated = gate_val * sig
        gate_share = gate_share + jnp.sum(returned * (activated * up_val), axis=1, keepdims=True)
        d_hidden = gate * returned
        d_gate_tile = (d_hidden * up_val * sig * (1.0 + gate_val * (1.0 - sig))).astype(bf16)
        d_up_tile = (d_hidden * activated).astype(bf16)
        d_gate[:, here] = d_gate_tile
        d_up[:, here] = d_up_tile
        share_gate = share_gate + dot(d_gate_tile, adapt_out[0, :, here], 1, 1)
        share_up = share_up + dot(d_up_tile, adapt_out[1, :, here], 1, 1)
        added = dot(d_gate_tile, gate_mat[:, here], 1, 1) + dot(d_up_tile, up_mat[:, here], 1, 1)
        if step == 0:
            d_rows[...] = added
        else:
            d_rows[...] += added
    share = adapter_scale * jnp.concatenate([share_gate, share_up], axis=1)

    high = share.astype(bf16)
    low = (share - high.astype(f32)).astype(bf16)
    all_rows = d_rows[...] + dot(high, adapt[...], 1, 0) + dot(low, adapt[...], 1, 0)
    all_rows = all_rows + (gate_share * slope) * dot(signs.astype(bf16), router[...], 1, 0)

    token_grads = dot(dispatch, all_rows.astype(bf16), 0, 0).astype(bf16)
    lanes = part_rows * rank2
    flat = dot(high, spread(rank2, part_rows), 1, 0)
    mine = lax.div(iota((rows, lanes), 1), rank2) == lax.rem(iota((rows, lanes), 0), part_rows)
    flat = jnp.where(mine, flat, 0.0).astype(bf16)
    target, source = iota((devices, rows), 0), iota((devices, rows), 1)
    to_expert = lax.rem(lax.div(target, tensor_size), expert_size) == expert
    source_part = jnp.where(source < part_rows, part, 1 - part)
    to_part = lax.div(target, tensor_size * expert_size) == source_part
    goes = jnp.where(to_expert & to_part, 1.0, 0.0).astype(bf16)
    latent_grads = dot(goes, flat, 1, 0).astype(bf16)
    half, half_lanes = width // 2, lanes // 2
    out[:, 0, :] = jnp.concatenate([token_grads[:, :half], latent_grads[:, :half_lanes]], axis=1)
    out[:, 1, :] = jnp.concatenate([token_grads[:, half:], latent_grads[:, half_lanes:]], axis=1)

    d_gate_all, d_up_all = d_gate[...].astype(f32), d_up[...].astype(f32)
    for ref, first in ((kept, 0), (sent, part_rows)):
        rows_of = slice(first, first + part_rows)
        ref[...] = jnp.concatenate([d_gate_all[rows_of], d_up_all[rows_of]], axis=0).astype(bf16)
    own_x[...] = slot_x[:part_rows, :width].astype(bf16)
    own_latent[...] = latent.astype(f32)[:part_rows].astype(bf16)


def up_kernel(kept, received, latent, out):
    part = lax.axis_index("parts")
    rows, rank2 = latent.shape
    hidden = kept.shape[1]
    rank = rank2 // 2
    for ref, number in ((kept, part), (received, 1 - part)):
        cols = pl.ds(pl.multiple_of(number * hidden, hidden), hidden)
        for side in range(2):
            out[side, :, cols] = adapter_scale * dot(
                latent[:, side * rank : (side + 1) * rank],
                ref[side * rows : (side + 1) * rows, :],
                0,
                0,
            )


def last_kernel(received, x_cols, grad_tokens, grad_down):
    rank2, cols = grad_down.shape
    width = grad_tokens.shape[1]
    half = width // 2
    if x_cols.shape[1] == cols:
        x = x_cols[...]
    else:
        x = x_cols[:, pl.ds(pl.multiple_of(lax.axis_index("tensor") * cols, cols), cols)]
    rows = x.shape[0]
    total = jnp.sum(received[...].astype(f32), axis=0)
    grad_tokens[...] = jnp.concatenate([total[0:1, :half], total[1:2, :half]], axis=1).astype(bf16)
    flat = jnp.concatenate([total[0:1, half:], total[1:2, half:]], axis=1)
    lanes = rows * rank2
    mine = lax.div(iota((rows, lanes), 1), rank2) == iota((rows, lanes), 0)
    d_latent = dot(jnp.where(mine, flat, 0.0).astype(bf16), spread(rank2, rows), 1, 1).astype(bf16)
    grad_down[...] = dot(d_latent, x, 0, 0)


def per_device(tokens, cotangent, routes, router, w_gate, w_up, w_down, adapter_down, adapter_up):
    parts, expert_size = lax.axis_size("parts"), lax.axis_size("expert")
    tensor_size = lax.axis_size("tensor")
    devices = parts * expert_size * tensor_size
    size_group, experts = routes.shape[0], router.shape[1]
    capacity = 2 * size_group // experts * 5 // 4
    width = tokens.shape[1]
    hidden = w_gate.shape[2] // parts
    rank2 = adapter_down.shape[2]
    col_width = adapter_down.shape[1]
    part_rows = expert_size * capacity
    rows = parts * part_rows
    tile = min(hidden, 512)
    tiles = hidden // tile
    lanes = part_rows * rank2

    adapt_in = adapter_down[0].T
    by_flip = tensor_size == 4 and col_width % 128 == 0

    if by_flip:
        cuts = width // col_width
        bundle_rows = rank2 + -(-2 * cuts // 16) * 16
        bundle = pl.pallas_call(
            bundle_kernel,
            out_shape=jax.ShapeDtypeStruct((bundle_rows, col_width), bf16),
            in_specs=[hbm] * 3,
            out_specs=vmem,
            scratch_shapes=[pltpu.VMEM((2, 1, width), bf16), pltpu.SemaphoreType.DMA((3,))],
            compiler_params=pltpu.CompilerParams(vmem_limit_bytes=2 * mib),
            name="bundle",
        )(in_hbm(tokens), in_hbm(cotangent), in_hbm(adapt_in))
        pieces = [bundle] + [
            lax.ppermute(bundle, "tensor", [(i, i ^ flip) for i in range(tensor_size)])
            for flip in range(1, tensor_size)
        ]
        group_rows = pieces
    else:
        pieces = [lax.all_gather(adapt_in, "tensor", axis=1, tiled=True)]
        group_rows = [
            lax.all_gather(rows, "tensor", axis=0, tiled=True) for rows in (tokens, cotangent)
        ] + pieces
    gate_half, router_near, adapt_out_near = fetch(w_gate, router.T, adapter_up[0], hidden)

    def pack(*refs):
        inputs, outputs = refs[: 1 + len(group_rows)], refs[2 + len(group_rows) :]
        pack_kernel(
            capacity, rank2, len(pieces), *inputs, outputs[:experts], *outputs[experts:]
        )

    *packed, adapt = pl.pallas_call(
        pack,
        out_shape=(
            *(jax.ShapeDtypeStruct((2 * capacity, width + extra), bf16),) * experts,
            jax.ShapeDtypeStruct((rank2, width), bf16),
        ),
        in_specs=[hbm] + [vmem] * (1 + len(group_rows)),
        out_specs=[vmem] * (experts + 1),
        scratch_shapes=[
            pltpu.SMEM(routes.shape[::-1], jnp.int32),
            pltpu.SemaphoreType.DMA,
        ],
        compiler_params=pltpu.CompilerParams(vmem_limit_bytes=16 * mib),
        name="pack",
    )(in_hbm(routes.T), *group_rows, pltpu.with_memory_space_constraint(gate_half, pltpu.VMEM))
    plane = range(parts * experts)
    slots = [packed[0]] + [
        lax.ppermute(packed[flip % experts], ("parts", "expert"), [(i, i ^ flip) for i in plane])
        for flip in plane
        if flip > 0
    ]
    sizes = (tensor_size, expert_size, size_group, capacity, devices, tile)

    def main(*refs):
        main_kernel(sizes, refs[: len(slots)], *refs[len(slots) :])

    out, sent, kept, own_x, own_latent = pl.pallas_call(
        main,
        out_shape=(
            jax.ShapeDtypeStruct((devices, 2, (width + lanes) // 2), bf16),
            jax.ShapeDtypeStruct((2 * part_rows, hidden), bf16),
            jax.ShapeDtypeStruct((2 * part_rows, hidden), bf16),
            jax.ShapeDtypeStruct((part_rows, width), bf16),
            jax.ShapeDtypeStruct((part_rows, rank2), bf16),
        ),
        in_specs=[vmem] * (len(slots) + 4) + [hbm] * 2,
        out_specs=[vmem] * 5,
        scratch_shapes=[
            pltpu.VMEM((width, hidden), bf16),
            pltpu.VMEM((hidden, width), bf16),
            pltpu.VMEM((rows, hidden), f32),
            pltpu.VMEM((rows, hidden), bf16),
            pltpu.VMEM((rows, hidden), bf16),
            pltpu.VMEM((rows, width), f32),
            pltpu.SemaphoreType.DMA((2, tiles)),
        ],
        cost_estimate=pl.CostEstimate(
            flops=10 * rows * width * hidden,
            bytes_accessed=2 * width * hidden,
            transcendentals=rows * hidden,
        ),
        compiler_params=pltpu.CompilerParams(vmem_limit_bytes=38 * mib),
        name="main",
    )(
        *slots,
        adapt,
        pltpu.with_memory_space_constraint(gate_half, pltpu.VMEM),
        *[
            pltpu.with_memory_space_constraint(near, pltpu.VMEM)
            for near in (router_near, adapt_out_near)
        ],
        in_hbm(w_up),
        in_hbm(w_down),
    )

    received = lax.all_to_all(out, every_axis, split_axis=0, concat_axis=0, tiled=True)
    other = lax.ppermute(sent, "parts", [(0, 1), (1, 0)])
    grad_up = pl.pallas_call(
        up_kernel,
        out_shape=jax.ShapeDtypeStruct(adapter_up.shape[1:], f32),
        in_specs=[vmem] * 3,
        out_specs=vmem,
        cost_estimate=pl.CostEstimate(
            flops=8 * part_rows * rank2 * hidden,
            bytes_accessed=8 * rank2 * hidden,
            transcendentals=0,
        ),
        compiler_params=pltpu.CompilerParams(vmem_limit_bytes=16 * mib),
        name="grad_up",
    )(kept, other, own_latent)

    if col_width % 128 == 0:
        x_cols = own_x
    else:
        x_cols = lax.dynamic_slice_in_dim(
            own_x, lax.axis_index("tensor") * col_width, col_width, 1
        )
    grad_tokens, grad_down = pl.pallas_call(
        last_kernel,
        out_shape=(
            jax.ShapeDtypeStruct(tokens.shape, bf16),
            jax.ShapeDtypeStruct((rank2, col_width), f32),
        ),
        in_specs=[vmem] * 2,
        out_specs=[vmem] * 2,
        compiler_params=pltpu.CompilerParams(vmem_limit_bytes=40 * mib),
        name="last",
    )(received, x_cols)
    return (grad_tokens, grad_down.T[None], grad_up[None])


def solution(mesh):
    return jax.shard_map(
        per_device,
        mesh=mesh,
        in_specs=(
            P(every_axis, None),
            P(every_axis, None),
            P(("parts", "expert"), None),
            P(),
            P("expert", None, "tensor"),
            P("expert", None, "tensor"),
            P("expert", "tensor", None),
            P("expert", "tensor", None),
            P("expert", None, None, "tensor"),
        ),
        out_specs=(
            P(every_axis, None),
            P(("parts", "expert"), "tensor", None),
            P(("parts", "expert"), None, None, "tensor"),
        ),
        check_vma=False,
    )
```
